32 devices in a mesh: rep: 2 (over x), lat: 16 (over z, y, core).
Axes of the slice: x: 2, y: 2, z: 4, core: 2. Of those that a mesh axis runs over, the one named last changes fastest.
Arguments:
- residuals: bfloat16 [512, 2, 3584], P(('rep', 'lat')), parts along dimension 0, may hold values from -6 to 6
- enc_weight: bfloat16 [2, 3584, 16384], P(None, None, 'lat'), may hold values from -0.09375 to 0.09375
- enc_bias: float32 [2, 16384], P(None, 'lat'), may hold values from -1 to 0.5
- dec_weight: bfloat16 [3, 16384, 3584], P(None, 'lat'), may hold values from -0.125 to 0.125
- dec_bias: float32 [2, 3584], replicated, may hold values from -3 to 3
- active_blocks: int32 [4, 4, 32], P('rep'), parts along dimension 0, may hold values from 0 to 127, as said below
- active_counts: int32 [4, 4], P('rep'), parts along dimension 0, may hold values from 1 to 32, as said below
Outputs:
- recon: bfloat16 [512, 2, 3584], P(('rep', 'lat')), parts along dimension 0
The draws below stay inside these ranges and needn't reach their ends.
There are 2 independent parts, one for each index of `rep`. The reference program is written for one: setup_inputs(seed, part) draws one part's arguments, and reference() takes and returns one part's arrays. A program takes and returns all parts, laid end to end along the dimension named above; an argument that names none is the same for every part. Nothing has to cross between parts.
Inputs may be any that keep to these rules, and one draw needn't show every extreme that they name: `active_blocks`: the first active_counts entries of each layer's tile list are distinct latent blocks; later entries are to be ignored. `active_counts`: some layer's tile uses all 32 entries.
All inputs are finite; a program needn't handle non-finite values.
Results may differ from the reference program's by a relative error of at most 0.0046.
Values may be sent and summed in bfloat16 or wider, within the bound.
A program may use at most 128 MiB of HBM per device.

```python
import jax
import jax.numpy as jnp

D = 3584
LATENTS = 16384
BLOCK = 128
LAYERS = 2
TILE = 64
KMAX = 32
TILES = 4
TOKENS = 256
NB = 128
PAIRS = 3


def draw_active_blocks(key, part):
    key = jax.random.fold_in(key, 11)
    subkeys = jax.random.split(key, LAYERS * TILES)
    orders = jax.vmap(lambda single: jax.random.permutation(single, NB))(subkeys)
    return orders[:, :KMAX].reshape(LAYERS, TILES, KMAX).astype(jnp.int32)


def draw_active_counts(key, part):
    key = jax.random.fold_in(key, 23)
    first, second = jax.random.split(key)
    counts = jax.random.randint(first, (LAYERS * TILES,), 1, KMAX + 1)
    position = jax.random.randint(second, (), 0, LAYERS * TILES)
    counts = counts.at[position].set(KMAX)
    return counts.reshape(LAYERS, TILES).astype(jnp.int32)


def level_of(stream_key, shape, cuts, low, top_value):
    loudness = 1.0
    for dim, shards_of in cuts:
        steps = jax.random.uniform(jax.random.fold_in(jax.random.fold_in(stream_key, 6), dim), (shards_of,), jnp.float32, low / len(cuts), top_value / len(cuts))
        loudness = loudness * jnp.repeat(jnp.exp(steps), shape[dim] // shards_of).reshape((-1,) + (1,) * (len(shape) - 1 - dim))
    return loudness


def normal_values(own_key, dims, width, bound, pieces=(), held_as=jnp.bfloat16):
    level = level_of(own_key, dims, pieces, -0.22, 0.18) if pieces else 1.0
    array = jax.random.normal(own_key, dims, jnp.float32) * width * level
    return jnp.minimum(jnp.maximum(array, -bound), bound).astype(held_as)


def setup_inputs(seed: int = 0, part: int = 0) -> dict:
    arg_keys = jax.random.split(jax.random.key(seed), 8)
    own_keys = jax.random.split(jax.random.fold_in(arg_keys[7], part), 8)
    residuals = normal_values(own_keys[0], (TOKENS, LAYERS, D), 1.0, 6.0, ((0, 16),))
    enc_weight = normal_values(arg_keys[1], (LAYERS, D, LATENTS), D ** -0.5, 0.09375, ((2, 16),))
    enc_bias = jnp.clip(-1.0 + 1.5 * jax.random.uniform(arg_keys[2], (LAYERS, LATENTS), jnp.float32) ** level_of(arg_keys[2], (LAYERS, LATENTS), ((1, 16),), -0.2, 0.2), -1.0, 0.5)
    dec_weight = normal_values(arg_keys[3], (PAIRS, LATENTS, D), (KMAX * BLOCK // 2) ** -0.5, 0.125, ((1, 16),))
    dec_bias = normal_values(arg_keys[4], (LAYERS, D), 0.5, 3.0, (), jnp.float32)
    active_blocks = draw_active_blocks(jax.random.fold_in(jax.random.fold_in(arg_keys[7], part), 71), part)
    active_counts = draw_active_counts(jax.random.fold_in(jax.random.fold_in(arg_keys[7], part), 71), part)
    return {"residuals": residuals, "enc_weight": enc_weight, "enc_bias": enc_bias, "dec_weight": dec_weight, "dec_bias": dec_bias, "active_blocks": active_blocks, "active_counts": active_counts}


def pair_index(source, target):
    return source * LAYERS - source * (source - 1) // 2 + target - source


def reference(residuals, enc_weight, enc_bias, dec_weight, dec_bias, active_blocks, active_counts):
    in_list = jnp.arange(KMAX, dtype=jnp.int32)[None, None, :] < active_counts[:, :, None]
    block_ids = jnp.arange(NB, dtype=jnp.int32)
    active = jnp.any((active_blocks[..., None] == block_ids) & in_list[..., None], axis=2)
    active_rows = jnp.repeat(active.astype(jnp.float32), TILE, axis=1)
    latent_codes = []
    for source in range(LAYERS):
        preact = jnp.dot(residuals[:, source, :], enc_weight[source], preferred_element_type=jnp.float32)
        preact = preact + enc_bias[source][None, :]
        activation = jax.nn.relu(preact).reshape(TOKENS, NB, BLOCK) * active_rows[source][:, :, None]
        latent_codes.append(activation.reshape(TOKENS, LATENTS).astype(jnp.bfloat16))
    outputs = []
    for target in range(LAYERS):
        summed = jnp.zeros((TOKENS, D), jnp.float32)
        for source in range(target + 1):
            summed = summed + jnp.dot(latent_codes[source], dec_weight[pair_index(source, target)], preferred_element_type=jnp.float32)
        outputs.append((summed + dec_bias[target][None, :]).astype(jnp.bfloat16))
    return jnp.stack(outputs, axis=1)
```

```python
import functools

import jax
import jax.numpy as jnp
from jax import lax
from jax.experimental import pallas as pl
from jax.experimental.pallas import tpu as pltpu
from jax.sharding import PartitionSpec as P

BLOCK = 128
LAYERS = 2
TILE = 64
CORES = 2
YS = 2
CHUNK = 256
HALVES = 2
MESH = pl.DeviceIdType.MESH


def pair_index(source, target):
    return source * LAYERS - source * (source - 1) // 2 + target - source


def fused(
    zs, x_ref, ew_hbm, eb_ref, dw_hbm, db_ref, ab_ref, ac_ref, o_ref,
    ew, dw, xg, codes, mask, acc, csend, crecv, ysend, yrecv, zsend, zrecv,
    w_sem, up_sem, down_sem, y_sem, core_sem, got_sem,
    cs_sem, cr_sem, ys_sem, yr_sem, zs_sem, zr_sem,
):
    layers, rows, width = x_ref.shape
    lat_here = ew.shape[2]
    seg_cols = acc.shape[2]
    half = width // seg_cols
    plane = zs * rows
    kept = YS * plane
    f32, bf16 = jnp.float32, jnp.bfloat16

    rep = lax.axis_index("rep")
    me = lax.axis_index("lat")
    core = lax.rem(me, CORES)
    y = lax.rem(me // CORES, YS)
    z = me // (CORES * YS)

    def device(z_at, y_at, core_at):
        return (rep, (z_at * YS + y_at) * CORES + core_at)

    up, down = device(z + 1, y, core), device(z - 1, y, core)
    across, twin = device(z, 1 - y, core), device(z, y, 1 - core)
    has_up, has_down = z < zs - 1, z > 0

    barrier = pltpu.get_barrier_semaphore()
    for peer in (across, twin):
        pl.semaphore_signal(barrier, inc=1, device_id=peer, device_id_type=MESH)

    @pl.when(has_up)
    def _():
        pl.semaphore_signal(barrier, inc=1, device_id=up, device_id_type=MESH)

    @pl.when(has_down)
    def _():
        pl.semaphore_signal(barrier, inc=1, device_id=down, device_id_type=MESH)

    def weight_copies():
        copies = [pltpu.make_async_copy(ew_hbm.at[l], ew.at[l], w_sem.at[l]) for l in range(layers)]
        copies += [
            pltpu.make_async_copy(dw_hbm.at[p], dw.at[p], w_sem.at[layers + p])
            for p in range(dw.shape[0])
        ]
        return copies

    weights = weight_copies()
    order = [0, layers, 1] + [layers + p for p in range(1, dw.shape[0])]
    for i in order:
        weights[i].start()

    for l in range(layers):
        xg[l, pl.ds(pl.multiple_of(z * rows, rows), rows), :] = x_ref[l]

    pl.semaphore_wait(
        barrier, 2 + jnp.where(has_up, 1, 0) + jnp.where(has_down, 1, 0)
    )

    def at(l, slot):
        return xg.at[l, pl.ds(pl.multiple_of(slot * rows, rows), rows), :]

    def gather_copy(l, slot, to_slot, peer, send_sem):
        return pltpu.make_async_remote_copy(
            src_ref=at(l, slot), dst_ref=at(l, to_slot), send_sem=send_sem,
            recv_sem=got_sem.at[l, to_slot], device_id=peer, device_id_type=MESH,
        )

    def up_copy(l, zb):
        return gather_copy(l, zb, zb, up, up_sem.at[l, zb])

    def down_copy(l, zb):
        return gather_copy(l, zb, zb, down, down_sem.at[l, zb])

    def y_copy(l, zb):
        return gather_copy(l, zb, zs + zb, across, y_sem.at[l, zb])

    def core_copy(l, slot):
        return gather_copy(l, slot, 2 * zs + slot, twin, core_sem.at[l, slot])

    def got(l, slot):
        pltpu.make_async_remote_copy(
            src_ref=at(l, slot), dst_ref=at(l, slot), send_sem=core_sem.at[l, 0],
            recv_sem=got_sem.at[l, slot], device_id=twin, device_id_type=MESH,
        ).wait_recv()

    def own(l):
        y_copy(l, z).start()

        @pl.when(has_up)
        def _():
            up_copy(l, z).start()

        @pl.when(has_down)
        def _():
            down_copy(l, z).start()

        core_copy(l, z).start()

    def step(l, s):
        @pl.when(z >= s)
        def _():
            zb = z - s
            got(l, zb)

            @pl.when(has_up)
            def _():
                up_copy(l, zb).start()

            y_copy(l, zb).start()
            core_copy(l, zb).start()

        @pl.when(z + s < zs)
        def _():
            zb = z + s
            got(l, zb)

            @pl.when(has_down)
            def _():
                down_copy(l, zb).start()

            y_copy(l, zb).start()
            core_copy(l, zb).start()

    def y_forward(l, s):
        @pl.when(z >= s)
        def _():
            got(l, zs + z - s)
            core_copy(l, zs + z - s).start()

        if s:
            @pl.when(z + s < zs)
            def _():
                got(l, zs + z + s)
                core_copy(l, zs + z + s).start()

    def y_forwards(l):
        for s in range(zs):
            y_forward(l, s)

    def core_gets(l):
        for slot in range(2 * zs, 4 * zs):
            got(l, slot)

    def make_mask():
        for l in range(layers):
            listed = ab_ref[l]
            tile = lax.broadcasted_iota(jnp.int32, listed.shape, 0)
            place = lax.broadcasted_iota(jnp.int32, listed.shape, 1)
            count = jnp.zeros(listed.shape, jnp.int32)
            for t in range(zs):
                count = jnp.where(tile == t, ac_ref[l, t], count)
            used = place < count
            blocks_here = lat_here // BLOCK
            for j in range(blocks_here):
                hit = jnp.where(used & (listed == me * blocks_here + j), 1.0, 0.0)
                hit = jnp.max(hit, axis=1, keepdims=True)
                for t in range(zs):
                    mask[l, t * rows : (t + 1) * rows, j * BLOCK : (j + 1) * BLOCK] = (
                        jnp.broadcast_to(hit[t : t + 1], (rows, BLOCK))
                    )

    def encode(l, first, last):
        @pl.loop(first, last)
        def _(n):
            cols = pl.ds(pl.multiple_of(n * CHUNK, CHUNK), CHUNK)
            pre = jnp.dot(xg[l], ew[l, :, cols], preferred_element_type=f32)
            pre = jnp.maximum(pre + eb_ref[l : l + 1, cols], 0.0)
            pre = pre.reshape(CORES * YS, plane, CHUNK) * mask[l, :, cols][None]
            codes[l, :, cols] = pre.reshape(CORES * kept, CHUNK).astype(bf16)

    def decode(seg):
        m, h = seg // half, seg % half

        @pl.loop(0, seg_cols // CHUNK)
        def _(j):
            cols = pl.ds(pl.multiple_of(h * seg_cols + j * CHUNK, CHUNK), CHUNK)
            to = pl.ds(pl.multiple_of(j * CHUNK, CHUNK), CHUNK)
            total = None
            for l in range(m + 1):
                term = jnp.dot(
                    codes[l], dw[pair_index(l, m), :, cols], preferred_element_type=f32
                )
                total = term if total is None else total + term
            acc[seg, :, to] = total[:kept]
            csend[seg, :, to] = total[kept:].astype(bf16)

        core_sum(seg).start()

    def core_sum(seg):
        return pltpu.make_async_remote_copy(
            src_ref=csend.at[seg], dst_ref=crecv.at[seg], send_sem=cs_sem.at[seg],
            recv_sem=cr_sem.at[seg], device_id=twin, device_id_type=MESH,
        )

    def y_sum(seg):
        return pltpu.make_async_remote_copy(
            src_ref=ysend.at[seg], dst_ref=yrecv.at[seg], send_sem=ys_sem.at[seg],
            recv_sem=yr_sem.at[seg], device_id=across, device_id_type=MESH,
        )

    def z_sum(seg, way, d):
        part = pl.ds(pl.multiple_of(d * rows, rows), rows)
        return pltpu.make_async_remote_copy(
            src_ref=zsend.at[seg, part], dst_ref=zrecv.at[seg, way, part],
            send_sem=zs_sem.at[seg, d], recv_sem=zr_sem.at[seg, way, d],
            device_id=(up, down)[way], device_id_type=MESH,
        )

    def after_core(seg):
        core_sum(seg).wait_recv()
        ysend[seg] = (acc[seg, plane:] + crecv[seg, plane:].astype(f32)).astype(bf16)
        y_sum(seg).start()
        acc[seg, :plane] = acc[seg, :plane] + crecv[seg, :plane].astype(f32)

    def after_y(seg):
        y_sum(seg).wait_recv()
        acc[seg, :plane] = acc[seg, :plane] + yrecv[seg].astype(f32)

    def take(seg, way, d):
        part = pl.ds(pl.multiple_of(d * rows, rows), rows)
        z_sum(seg, way, d).wait_recv()
        acc[seg, part] = acc[seg, part] + zrecv[seg, way, part].astype(f32)

    def z_hop(seg, way, d):
        part = pl.ds(d * rows, rows)
        going, chained = ((z < d, has_down), (z > d, has_up))[way]

        @pl.when(going)
        def _():
            @pl.when(chained)
            def _():
                take(seg, way, d)

            zsend[seg, part] = acc[seg, part].astype(bf16)
            z_sum(seg, way, d).start()

    def z_hops(seg):
        for i in range(1, zs):
            z_hop(seg, 0, zs - i)
            z_hop(seg, 1, i - 1)

    def finish(seg):
        @pl.when(has_down)
        def _():
            take(seg, 0, z)

        @pl.when(has_up)
        def _():
            take(seg, 1, z)

        m, h = seg // half, seg % half
        cols = slice(h * seg_cols, (h + 1) * seg_cols)
        own_rows = pl.ds(pl.multiple_of(z * rows, rows), rows)
        o_ref[m, :, cols] = (acc[seg, own_rows] + db_ref[m : m + 1, cols]).astype(bf16)

    chunks = lat_here // CHUNK
    mid = (chunks + 1) // 2
    own(0)
    make_mask()
    step(0, 1)
    step(0, 2)
    own(1)
    step(0, 3)
    y_forwards(0)
    step(1, 1)
    core_gets(0)
    weights[0].wait()
    encode(0, 0, mid)
    step(1, 2)
    encode(0, mid, chunks)
    step(1, 3)
    weights[layers].wait()
    decode(0)
    y_forwards(1)
    after_core(0)
    decode(1)
    core_gets(1)
    after_core(1)
    weights[1].wait()
    encode(1, 0, chunks)
    after_y(0)
    for p in range(1, dw.shape[0]):
        weights[layers + p].wait()
    decode(2)
    after_y(1)
    after_core(2)
    z_hops(0)
    decode(3)
    z_hops(1)
    after_core(3)
    finish(0)
    after_y(2)
    z_hops(2)
    finish(1)
    after_y(3)
    z_hops(3)
    finish(2)
    finish(3)

    for l in range(layers):
        for zb in range(zs):
            @pl.when(has_up & (z >= zb))
            def _():
                up_copy(l, zb).wait_send()

            @pl.when(has_down & (z <= zb))
            def _():
                down_copy(l, zb).wait_send()

            y_copy(l, zb).wait_send()
        for slot in range(2 * zs):
            core_copy(l, slot).wait_send()
    for seg in range(layers * half):
        core_sum(seg).wait_send()
        y_sum(seg).wait_send()
        for d in range(zs):
            for way in range(2):
                @pl.when((z < d, z > d)[way])
                def _():
                    z_sum(seg, way, d).wait_send()


def body_fused(zs, residuals, enc_weight, enc_bias, dec_weight, dec_bias, active_blocks, active_counts):
    rows, layers, width = residuals.shape
    lat_here = enc_weight.shape[2]
    pairs = dec_weight.shape[0]
    segs, seg_cols = layers * HALVES, width // HALVES
    slots = CORES * YS * zs
    plane = zs * rows
    kept = YS * plane
    bf16, f32 = jnp.bfloat16, jnp.float32
    vmem = pl.BlockSpec(memory_space=pltpu.VMEM)
    hbm = pl.BlockSpec(memory_space=pl.ANY)
    dma = pltpu.SemaphoreType.DMA
    out = pl.pallas_call(
        functools.partial(fused, zs),
        out_shape=jax.ShapeDtypeStruct((layers, rows, width), bf16),
        in_specs=[vmem, hbm, vmem, hbm, vmem, vmem, pl.BlockSpec(memory_space=pltpu.SMEM)],
        out_specs=vmem,
        scratch_shapes=[
            pltpu.VMEM((layers, width, lat_here), bf16),
            pltpu.VMEM((pairs, lat_here, width), bf16),
            pltpu.VMEM((layers, slots * rows, width), bf16),
            pltpu.VMEM((layers, slots * rows, lat_here), bf16),
            pltpu.VMEM((layers, plane, lat_here), f32),
            pltpu.VMEM((segs, kept, seg_cols), f32),
            pltpu.VMEM((segs, kept, seg_cols), bf16),
            pltpu.VMEM((segs, kept, seg_cols), bf16),
            pltpu.VMEM((segs, plane, seg_cols), bf16),
            pltpu.VMEM((segs, plane, seg_cols), bf16),
            pltpu.VMEM((segs, plane, seg_cols), bf16),
            pltpu.VMEM((segs, 2, plane, seg_cols), bf16),
            dma((layers + pairs,)),
            dma((layers, zs)),
            dma((layers, zs)),
            dma((layers, zs)),
            dma((layers, 2 * zs)),
            dma((layers, slots)),
            dma((segs,)),
            dma((segs,)),
            dma((segs,)),
            dma((segs,)),
            dma((segs, zs)),
            dma((segs, 2, zs)),
        ],
        compiler_params=pltpu.CompilerParams(
            collective_id=0, has_side_effects=True, vmem_limit_bytes=61 * 2**20
        ),
    )(
        residuals.transpose(1, 0, 2), enc_weight, enc_bias, dec_weight, dec_bias,
        active_blocks, active_counts,
    )
    return out.transpose(1, 0, 2)


def block_table(active_blocks, active_counts, blocks_here):
    holder = lax.axis_index("lat")
    block_ids = holder * blocks_here + jnp.arange(blocks_here, dtype=jnp.int32)
    in_list = (
        jnp.arange(active_blocks.shape[2], dtype=jnp.int32)[None, None, :]
        < active_counts[:, :, None]
    )
    matched = (active_blocks[..., None] == block_ids) & in_list[..., None]
    return jnp.any(matched, axis=2).astype(jnp.float32)


def encode(fragment, enc_weight, enc_bias, table):
    row_count = fragment.shape[0]
    lat_here = enc_weight.shape[2]
    blocks_here = lat_here // BLOCK
    preact = jnp.einsum("rld,ldk->rlk", fragment, enc_weight, preferred_element_type=jnp.float32)
    preact = preact + enc_bias[None, :, :]
    tile_of = jnp.arange(row_count, dtype=jnp.int32) // TILE
    one_hot = (tile_of[:, None] == jnp.arange(table.shape[1], dtype=jnp.int32)[None, :]).astype(
        jnp.float32
    )
    keep_rows = jnp.einsum("rt,ltj->rlj", one_hot, table)
    activation = (
        jax.nn.relu(preact).reshape(row_count, LAYERS, blocks_here, BLOCK) * keep_rows[..., None]
    )
    return activation.reshape(row_count, LAYERS, lat_here).astype(jnp.bfloat16)


def layer_term(latent_codes, dec_weight, target, amount):
    summed = jnp.zeros((amount, dec_weight.shape[2]), jnp.float32)
    for source in range(target + 1):
        summed = summed + jnp.dot(
            latent_codes[:, source, :],
            dec_weight[pair_index(source, target)],
            preferred_element_type=jnp.float32,
        )
    return summed


def body(residuals, enc_weight, enc_bias, dec_weight, dec_bias, active_blocks, active_counts):
    blocks_here = enc_weight.shape[2] // BLOCK
    table = block_table(active_blocks, active_counts, blocks_here)
    latent_codes = encode(
        lax.all_gather(residuals, "lat", axis=0, tiled=True), enc_weight, enc_bias, table
    )
    own_rows = latent_codes.shape[0] // lax.axis_size("lat")
    layers_out = []
    for target in range(LAYERS):
        layers_out.append(
            lax.psum_scatter(
                layer_term(latent_codes, dec_weight, target, own_rows * lax.axis_size("lat")),
                "lat",
                scatter_dimension=0,
                tiled=True,
            )
        )
    summed = jnp.stack(layers_out, axis=1)
    return (summed + dec_bias[None, :, :]).astype(jnp.bfloat16)


def solution(mesh):
    lat = mesh.shape["lat"]

    def either(residuals, enc_weight, *rest):
        rows = residuals.shape[0]
        zs = lat // (CORES * YS)
        whole = zs == 4 and rows % 16 == 0 and rows * CORES * YS == TILE
        part = functools.partial(body_fused, zs) if whole else body
        return part(residuals, enc_weight, *rest)

    return jax.shard_map(
        either,
        mesh=mesh,
        in_specs=(
            P(("rep", "lat"), None, None),
            P(None, None, "lat"),
            P(None, "lat"),
            P(None, "lat", None),
            P(),
            P("rep", None, None),
            P("rep", None),
        ),
        out_specs=P(("rep", "lat"), None, None),
        check_vma=False,
    )
```

```python
import functools

import jax
import jax.numpy as jnp
from jax import lax
from jax.experimental import pallas as pl
from jax.experimental.pallas import tpu as pltpu
from jax.sharding import PartitionSpec as P

BLOCK = 128
LAYERS = 2
TILE = 64
CORES = 2
YS = 2
CHUNK = 256
PIECES = ((0, 0, 2), (0, 1, 2), (1, 0, 2), (1, 1, 2))
SEGS = ((0, 0, 7), (0, 7, 7), (1, 0, 7), (1, 7, 7))
MESH = pl.DeviceIdType.MESH


def pair_index(source, target):
    return source * LAYERS - source * (source - 1) // 2 + target - source


def fused(
    zs, x_ref, ew_hbm, eb_ref, dw_hbm, db_ref, ab_ref, ac_ref, o_ref,
    ew, dw, xg, codes, mask, acc, csend, crecv, ysend, yrecv, zsend, zrecv,
    w_sem, line_sem, y_sem, core_sem, got_sem,
    cs_sem, cr_sem, ys_sem, yr_sem, zs_sem, zr_sem,
):
    layers, rows, width = x_ref.shape
    lat_here = ew.shape[2]
    plane = zs * rows
    kept = YS * plane
    f32, bf16 = jnp.float32, jnp.bfloat16

    rep = lax.axis_index("rep")
    me = lax.axis_index("lat")
    core = lax.rem(me, CORES)
    y = lax.rem(me // CORES, YS)
    z = me // (CORES * YS)

    def device(z_at, y_at, core_at):
        return (rep, (z_at * YS + y_at) * CORES + core_at)

    across, twin = device(z, 1 - y, core), device(z, y, 1 - core)

    def other(k):
        return (z + 1 - 2 * lax.rem(z, 2), lax.rem(z + 2, 4), 3 - z)[k]

    barrier = pltpu.get_barrier_semaphore()
    for peer in (across, twin, *(device(other(k), y, core) for k in range(3))):
        pl.semaphore_signal(barrier, inc=1, device_id=peer, device_id_type=MESH)

    def weight_copies():
        copies = [pltpu.make_async_copy(ew_hbm.at[l], ew.at[l], w_sem.at[l]) for l in range(layers)]
        copies += [
            pltpu.make_async_copy(dw_hbm.at[p], dw.at[p], w_sem.at[layers + p])
            for p in range(dw.shape[0])
        ]
        return copies

    weights = weight_copies()
    order = [0, layers, 1] + [layers + p for p in range(1, dw.shape[0])]
    for i in order:
        weights[i].start()

    for l in range(layers):
        xg[l, pl.ds(pl.multiple_of(z * rows, rows), rows), :] = x_ref[l]

    pl.semaphore_wait(barrier, 5)

    def at(q, slot):
        l, part, parts = PIECES[q]
        cols = width // parts
        return xg.at[
            l, pl.ds(pl.multiple_of(slot * rows, rows), rows), part * cols : (part + 1) * cols
        ]

    def gather_copy(q, slot, to_slot, peer, send_sem):
        return pltpu.make_async_remote_copy(
            src_ref=at(q, slot), dst_ref=at(q, to_slot), send_sem=send_sem,
            recv_sem=got_sem.at[q, to_slot], device_id=peer, device_id_type=MESH,
        )

    def line_copy(q, k):
        return gather_copy(q, z, z, device(other(k), y, core), line_sem.at[q, k])

    def y_copy(q, zb):
        return gather_copy(q, zb, zs + zb, across, y_sem.at[q, zb])

    def core_copy(q, slot):
        return gather_copy(q, slot, 2 * zs + slot, twin, core_sem.at[q, slot])

    def got(q, slot):
        pltpu.make_async_remote_copy(
            src_ref=at(q, slot), dst_ref=at(q, slot), send_sem=core_sem.at[q, 0],
            recv_sem=got_sem.at[q, slot], device_id=twin, device_id_type=MESH,
        ).wait_recv()

    def own(q):
        for k in reversed(range(3)):
            line_copy(q, k).start()
        y_copy(q, z).start()
        core_copy(q, z).start()

    def step(q, k):
        got(q, other(k))
        y_copy(q, other(k)).start()
        core_copy(q, other(k)).start()

    def y_forward(q, k):
        zb = z if k < 0 else other(k)
        got(q, zs + zb)
        core_copy(q, zs + zb).start()

    def core_gets(q):
        for slot in range(2 * zs, 4 * zs):
            got(q, slot)

    def make_mask():
        for l in range(layers):
            listed = ab_ref[l]
            tile = lax.broadcasted_iota(jnp.int32, listed.shape, 0)
            place = lax.broadcasted_iota(jnp.int32, listed.shape, 1)
            count = jnp.zeros(listed.shape, jnp.int32)
            for t in range(zs):
                count = jnp.where(tile == t, ac_ref[l, t], count)
            used = place < count
            blocks_here = lat_here // BLOCK
            for j in range(blocks_here):
                hit = jnp.where(used & (listed == me * blocks_here + j), 1.0, 0.0)
                hit = jnp.max(hit, axis=1, keepdims=True)
                for t in range(zs):
                    mask[l, t * rows : (t + 1) * rows, j * BLOCK : (j + 1) * BLOCK] = (
                        jnp.broadcast_to(hit[t : t + 1], (rows, BLOCK))
                    )

    def encode(l, first, last):
        @pl.loop(first, last)
        def _(n):
            cols = pl.ds(pl.multiple_of(n * CHUNK, CHUNK), CHUNK)
            pre = jnp.dot(xg[l], ew[l, :, cols], preferred_element_type=f32)
            pre = jnp.maximum(pre + eb_ref[l : l + 1, cols], 0.0)
            pre = pre.reshape(CORES * YS, plane, CHUNK) * mask[l, :, cols][None]
            codes[l, :, cols] = pre.reshape(CORES * kept, CHUNK).astype(bf16)

    def place(seg):
        m, first, count = SEGS[seg]
        return m * width + first * CHUNK, count * CHUNK

    def span(seg):
        return pl.ds(*place(seg))

    def rows_of(d):
        return pl.ds(pl.multiple_of(d * rows, rows), rows)

    def decode(seg):
        m, first, count = SEGS[seg]

        @pl.loop(first, first + count)
        def _(j):
            cols = pl.ds(pl.multiple_of(j * CHUNK, CHUNK), CHUNK)
            to = pl.ds(pl.multiple_of(m * width + j * CHUNK, CHUNK), CHUNK)
            total = None
            for l in range(m + 1):
                term = jnp.dot(
                    codes[l], dw[pair_index(l, m), :, cols], preferred_element_type=f32
                )
                total = term if total is None else total + term
            acc[:, to] = total[:kept]
            csend[:, to] = total[kept:].astype(bf16)

        core_sum(seg).start()

    def core_sum(seg):
        return pltpu.make_async_remote_copy(
            src_ref=csend.at[:, span(seg)], dst_ref=crecv.at[:, span(seg)],
            send_sem=cs_sem.at[seg], recv_sem=cr_sem.at[seg],
            device_id=twin, device_id_type=MESH,
        )

    def y_sum(seg):
        return pltpu.make_async_remote_copy(
            src_ref=ysend.at[:, span(seg)], dst_ref=yrecv.at[:, span(seg)],
            send_sem=ys_sem.at[seg], recv_sem=yr_sem.at[seg],
            device_id=across, device_id_type=MESH,
        )

    def z_sum(seg, k):
        return pltpu.make_async_remote_copy(
            src_ref=zsend.at[rows_of(other(k)), span(seg)], dst_ref=zrecv.at[k, :, span(seg)],
            send_sem=zs_sem.at[seg, k], recv_sem=zr_sem.at[seg, k],
            device_id=device(other(k), y, core), device_id_type=MESH,
        )

    def after_core(seg):
        core_sum(seg).wait_recv()
        cols = span(seg)
        ysend[:, cols] = (acc[plane:, cols] + crecv[plane:, cols].astype(f32)).astype(bf16)
        y_sum(seg).start()
        acc[:plane, cols] = acc[:plane, cols] + crecv[:plane, cols].astype(f32)

    def after_y(seg):
        y_sum(seg).wait_recv()
        cols = span(seg)
        total = acc[:plane, cols] + yrecv[:, cols].astype(f32)
        zsend[:, cols] = total.astype(bf16)
        for k in reversed(range(3)):
            z_sum(seg, k).start()
        acc[:plane, cols] = total

    def finish(seg):
        m, first, count = SEGS[seg]
        cols = span(seg)
        own_cols = slice(first * CHUNK, (first + count) * CHUNK)
        total = acc[rows_of(z), cols] + db_ref[m : m + 1, own_cols]
        for k in range(3):
            z_sum(seg, k).wait_recv()
            total = total + zrecv[k, :, cols].astype(f32)
        o_ref[m, :, own_cols] = total.astype(bf16)

    chunks = lat_here // CHUNK
    mid = (chunks + 1) // 2
    own(0)
    own(1)
    make_mask()
    for q in range(2):
        for k in range(3):
            step(q, k)
    own(2)
    own(3)
    for q in range(2):
        for k in range(-1, 3):
            y_forward(q, k)
    for k in range(3):
        step(2, k)
    for k in range(3):
        step(3, k)
    core_gets(0)
    core_gets(1)
    weights[0].wait()
    encode(0, 0, mid)
    for k in range(-1, 3):
        y_forward(2, k)
    encode(0, mid, chunks)
    weights[layers].wait()
    decode(0)
    for k in range(-1, 3):
        y_forward(3, k)
    after_core(0)
    decode(1)
    core_gets(2)
    core_gets(3)
    after_core(1)
    weights[1].wait()
    encode(1, 0, chunks)
    after_y(0)
    for p in range(1, dw.shape[0]):
        weights[layers + p].wait()
    decode(2)
    after_y(1)
    decode(3)
    after_core(2)
    after_core(3)
    finish(0)
    finish(1)
    after_y(2)
    after_y(3)
    finish(2)
    finish(3)

    for q in range(len(PIECES)):
        for k in range(3):
            line_copy(q, k).wait_send()
        for zb in range(zs):
            y_copy(q, zb).wait_send()
        for slot in range(2 * zs):
            core_copy(q, slot).wait_send()
    for seg in range(len(SEGS)):
        core_sum(seg).wait_send()
        y_sum(seg).wait_send()
        for k in range(3):
            z_sum(seg, k).wait_send()


def body_fused(zs, residuals, enc_weight, enc_bias, dec_weight, dec_bias, active_blocks, active_counts):
    rows, layers, width = residuals.shape
    lat_here = enc_weight.shape[2]
    pairs = dec_weight.shape[0]
    pieces, segs, total = len(PIECES), len(SEGS), layers * width
    slots = CORES * YS * zs
    plane = zs * rows
    kept = YS * plane
    bf16, f32 = jnp.bfloat16, jnp.float32
    vmem = pl.BlockSpec(memory_space=pltpu.VMEM)
    hbm = pl.BlockSpec(memory_space=pl.ANY)
    dma = pltpu.SemaphoreType.DMA
    out = pl.pallas_call(
        functools.partial(fused, zs),
        out_shape=jax.ShapeDtypeStruct((layers, rows, width), bf16),
        in_specs=[vmem, hbm, vmem, hbm, vmem, vmem, pl.BlockSpec(memory_space=pltpu.SMEM)],
        out_specs=vmem,
        scratch_shapes=[
            pltpu.VMEM((layers, width, lat_here), bf16),
            pltpu.VMEM((pairs, lat_here, width), bf16),
            pltpu.VMEM((layers, slots * rows, width), bf16),
            pltpu.VMEM((layers, slots * rows, lat_here), bf16),
            pltpu.VMEM((layers, plane, lat_here), f32),
            pltpu.VMEM((kept, total), f32),
            pltpu.VMEM((kept, total), bf16),
            pltpu.VMEM((kept, total), bf16),
            pltpu.VMEM((plane, total), bf16),
            pltpu.VMEM((plane, total), bf16),
            pltpu.VMEM((plane, total), bf16),
            pltpu.VMEM((3, rows, total), bf16),
            dma((layers + pairs,)),
            dma((pieces, 3)),
            dma((pieces, zs)),
            dma((pieces, 2 * zs)),
            dma((pieces, slots)),
            dma((segs,)),
            dma((segs,)),
            dma((segs,)),
            dma((segs,)),
            dma((segs, 3)),
            dma((segs, 3)),
        ],
        compiler_params=pltpu.CompilerParams(
            collective_id=0, has_side_effects=True, vmem_limit_bytes=61 * 2**20
        ),
    )(
        residuals.transpose(1, 0, 2), enc_weight, enc_bias, dec_weight, dec_bias,
        active_blocks, active_counts,
    )
    return out.transpose(1, 0, 2)


def block_table(active_blocks, active_counts, blocks_here):
    holder = lax.axis_index("lat")
    block_ids = holder * blocks_here + jnp.arange(blocks_here, dtype=jnp.int32)
    in_list = (
        jnp.arange(active_blocks.shape[2], dtype=jnp.int32)[None, None, :]
        < active_counts[:, :, None]
    )
    matched = (active_blocks[..., None] == block_ids) & in_list[..., None]
    return jnp.any(matched, axis=2).astype(jnp.float32)


def encode(fragment, enc_weight, enc_bias, table):
    row_count = fragment.shape[0]
    lat_here = enc_weight.shape[2]
    blocks_here = lat_here // BLOCK
    preact = jnp.einsum("rld,ldk->rlk", fragment, enc_weight, preferred_element_type=jnp.float32)
    preact = preact + enc_bias[None, :, :]
    tile_of = jnp.arange(row_count, dtype=jnp.int32) // TILE
    one_hot = (tile_of[:, None] == jnp.arange(table.shape[1], dtype=jnp.int32)[None, :]).astype(
        jnp.float32
    )
    keep_rows = jnp.einsum("rt,ltj->rlj", one_hot, table)
    activation = (
        jax.nn.relu(preact).reshape(row_count, LAYERS, blocks_here, BLOCK) * keep_rows[..., None]
    )
    return activation.reshape(row_count, LAYERS, lat_here).astype(jnp.bfloat16)


def layer_term(latent_codes, dec_weight, target, amount):
    summed = jnp.zeros((amount, dec_weight.shape[2]), jnp.float32)
    for source in range(target + 1):
        summed = summed + jnp.dot(
            latent_codes[:, source, :],
            dec_weight[pair_index(source, target)],
            preferred_element_type=jnp.float32,
        )
    return summed


def body(residuals, enc_weight, enc_bias, dec_weight, dec_bias, active_blocks, active_counts):
    blocks_here = enc_weight.shape[2] // BLOCK
    table = block_table(active_blocks, active_counts, blocks_here)
    latent_codes = encode(
        lax.all_gather(residuals, "lat", axis=0, tiled=True), enc_weight, enc_bias, table
    )
    own_rows = latent_codes.shape[0] // lax.axis_size("lat")
    layers_out = []
    for target in range(LAYERS):
        layers_out.append(
            lax.psum_scatter(
                layer_term(latent_codes, dec_weight, target, own_rows * lax.axis_size("lat")),
                "lat",
                scatter_dimension=0,
                tiled=True,
            )
        )
    summed = jnp.stack(layers_out, axis=1)
    return (summed + dec_bias[None, :, :]).astype(jnp.bfloat16)


def solution(mesh):
    lat = mesh.shape["lat"]

    def either(residuals, enc_weight, *rest):
        rows = residuals.shape[0]
        zs = lat // (CORES * YS)
        whole = zs == 4 and rows % 16 == 0 and rows * CORES * YS == TILE
        part = functools.partial(body_fused, zs) if whole else body
        return part(residuals, enc_weight, *rest)

    return jax.shard_map(
        either,
        mesh=mesh,
        in_specs=(
            P(("rep", "lat"), None, None),
            P(None, None, "lat"),
            P(None, "lat"),
            P(None, "lat", None),
            P(),
            P("rep", None, None),
            P("rep", None),
        ),
        out_specs=P(("rep", "lat"), None, None),
        check_vma=False,
    )
```
